32 devices in a mesh: row: 8 (over z, y), col: 4 (over x, core).
Axes of the slice: x: 2, y: 2, z: 4, core: 2. Of those that a mesh axis runs over, the one named last changes fastest.
Arguments:
- diag_block: float32 [256, 256], P(('row', 'col')), may hold values from -1 to 40, as said below
- panel: float32 [24576, 256], P(('row', 'col')), may hold values from -6 to 6
- trailing: bfloat16 [24576, 24576], P('row', 'col'), may hold values from -6 to 6
Outputs:
- diag_factor: float32 [256, 256], P(('row', 'col'))
- panel_factor: float32 [24576, 256], P(('row', 'col'))
- trailing_out: bfloat16 [24576, 24576], P('row', 'col')
The draws below stay inside these ranges and needn't reach their ends.
Inputs may be any that keep to these rules, and one draw needn't show every extreme that they name: diag_block is symmetric, with off-diagonal entries in -1 to 1 and diagonal entries in 24 to 40, so it is positive definite.
All inputs are finite; a program needn't handle non-finite values.
Results may differ from the reference program's by a relative error of at most 0.001.
Values sent between devices are 32-bit elements; how exact they have to be, the bound alone decides.
A program may use at most 128 MiB of HBM per device.

```python
import jax
import jax.numpy as jnp
from jax import lax

ORDER = 24576
PANEL = 256
BLOCK = 256
N_ROW = 8
N_COL = 4


def draw_diag_block(key, part):
    first_key, second_key = jax.random.split(key)
    entries = jax.random.uniform(first_key, (PANEL, PANEL), jnp.float32, -1.0, 1.0)
    balanced = 0.5 * (entries + entries.T)
    diag_values = jax.random.uniform(second_key, (PANEL,), jnp.float32, 24.0, 40.0)
    unit_diag = jnp.eye(PANEL, dtype=jnp.float32)
    return balanced * (1.0 - unit_diag) + unit_diag * diag_values[None, :]


def shard_levels(own_key, extent, cuts, low, largest):
    level = 1.0
    for dim, shards_of in cuts:
        draws = jax.random.uniform(jax.random.fold_in(jax.random.fold_in(own_key, 6), dim), (shards_of,), jnp.float32, low / len(cuts), largest / len(cuts))
        level = level * jnp.repeat(jnp.exp(draws), extent[dim] // shards_of).reshape((-1,) + (1,) * (len(extent) - 1 - dim))
    return level


def noise(own_key, extent, deviation, limit, pieces=(), kind=jnp.bfloat16):
    gain = shard_levels(own_key, extent, pieces, -0.22, 0.18) if pieces else 1.0
    result = jax.random.normal(own_key, extent, jnp.float32) * deviation * gain
    return jnp.minimum(jnp.maximum(result, -limit), limit).astype(kind)


def setup_inputs(seed: int = 0) -> dict:
    splits = jax.random.split(jax.random.key(seed), 4)
    return {
        "diag_block": draw_diag_block(jax.random.fold_in(splits[3], 71), 0),
        "panel": noise(splits[1], (ORDER, PANEL), 1.0, 6.0, ((0, 32),), jnp.float32),
        "trailing": noise(splits[2], (ORDER, ORDER), 1.0, 6.0, ((0, 8), (1, 4))),
    }


def reference(diag_block, panel, trailing):
    diag_factor = jnp.linalg.cholesky(diag_block)
    identity = jnp.eye(PANEL, dtype=jnp.float32)
    inverse = lax.linalg.triangular_solve(diag_factor, identity, left_side=True, lower=True)
    panel_factor = jnp.dot(panel.astype(jnp.float32), inverse.T.astype(jnp.float32), precision=lax.Precision.HIGHEST, preferred_element_type=jnp.float32)
    column_ratio = N_ROW // N_COL
    per_block = ORDER // N_ROW // BLOCK
    grouped = panel_factor.reshape(column_ratio, N_COL, per_block, BLOCK, PANEL)
    column_panel = jnp.transpose(grouped, (1, 2, 0, 3, 4)).reshape(ORDER, PANEL)
    row_step = min(ORDER, 512)
    stacked_rows = panel_factor.reshape(ORDER // row_step, row_step, PANEL)
    stacked_trailing = trailing.reshape(ORDER // row_step, row_step, ORDER)

    def one_block(operands):
        factor_rows, trailing_rows = operands
        update = jnp.dot(factor_rows.astype(jnp.float32), column_panel.T.astype(jnp.float32), precision=lax.Precision.HIGHEST, preferred_element_type=jnp.float32)
        return (trailing_rows.astype(jnp.float32) - update).astype(jnp.bfloat16)
    trailing_out = lax.map(one_block, (stacked_rows, stacked_trailing)).reshape(ORDER, ORDER)
    return (diag_factor, panel_factor, trailing_out)
```

```python
import functools

import jax
import jax.numpy as jnp
from jax import lax
from jax.experimental import pallas as pl
from jax.experimental.pallas import tpu as pltpu
from jax.sharding import PartitionSpec as P

BLOCK = 256
MIB = 1 << 20
MESH = pl.DeviceIdType.MESH


def split_three(x, axis, first):
    high = x.astype(jnp.bfloat16)
    low = (x - high.astype(jnp.float32)).astype(jnp.bfloat16)
    return jnp.concatenate([high, high, low] if first else [high, low, high], axis=axis)


def dot_last(a, b):
    return lax.dot_general(
        a, b, (((1,), (1,)), ((), ())), preferred_element_type=jnp.float32
    )


def gather_diag_kernel(n_row, n_col, mine, whole, held, send_sem, recv_sem):
    count = n_row * n_col
    me = lax.axis_index("row") * n_col + lax.axis_index("col")

    def target(step):
        other = lax.rem(me + step, count)
        return (other // n_col, lax.rem(other, n_col))

    barrier = pltpu.get_barrier_semaphore()

    def greet(step, carry):
        pl.semaphore_signal(barrier, inc=1, device_id=target(step), device_id_type=MESH)
        return carry

    lax.fori_loop(1, count, greet, 0)
    pl.semaphore_wait(barrier, count - 1)
    def send(step, carry):
        pltpu.make_async_remote_copy(
            src_ref=mine,
            dst_ref=held.at[me],
            send_sem=send_sem,
            recv_sem=recv_sem,
            device_id=target(step),
            device_id_type=MESH,
        ).start()
        return carry

    lax.fori_loop(1, count, send, 0)
    held[me] = mine[...]
    others = held.at[pl.ds(0, count - 1)]
    pltpu.make_async_copy(others, others, recv_sem).wait()
    pltpu.make_async_copy(others, others, send_sem).wait()
    whole[...] = held[...]


def gather_diag(diag_block, n_row, n_col):
    share, width = diag_block.shape
    whole = (n_row * n_col, share, width)
    gathered = pl.pallas_call(
        functools.partial(gather_diag_kernel, n_row, n_col),
        out_shape=jax.ShapeDtypeStruct(whole, jnp.float32),
        in_specs=[pl.BlockSpec(memory_space=pltpu.VMEM)],
        out_specs=pl.BlockSpec(memory_space=pltpu.VMEM),
        scratch_shapes=[
            pltpu.VMEM(whole, jnp.float32),
            pltpu.SemaphoreType.DMA,
            pltpu.SemaphoreType.DMA,
        ],
        compiler_params=pltpu.CompilerParams(collective_id=0, has_side_effects=True),
        cost_estimate=pl.CostEstimate(flops=0, bytes_accessed=16 * MIB, transcendentals=0),
        name="gather_diag",
    )(diag_block)
    return gathered.reshape(-1, width)


def eliminate(block, size):
    row_of = lax.broadcasted_iota(jnp.int32, (size, 2 * size), 0)
    col_of = lax.broadcasted_iota(jnp.int32, (size, 2 * size), 1)
    for j in range(size - 1):
        pivot_row = block[j : j + 1, :]
        scaled = pivot_row * (1.0 / block[j : j + 1, j : j + 1])
        factors = jnp.where(row_of > j, block[:, j : j + 1], 0.0)
        block = block - factors * scaled
    pivots = jnp.sum(jnp.where(row_of == col_of, block, 0.0), axis=1, keepdims=True)
    return block / jnp.sqrt(pivots)


def factor_kernel(diag, panel, lower, inverse, panel_factor, work):
    width = diag.shape[0]
    size = min(64, width)
    row_of = lax.broadcasted_iota(jnp.int32, (width, width), 0)
    col_of = lax.broadcasted_iota(jnp.int32, (width, width), 1)
    work[:, :width] = diag[...]
    work[:, width:] = jnp.where(row_of == col_of, 1.0, 0.0)
    eye = jnp.where(row_of == col_of, 1.0, 0.0)[:size, :size]
    for start in range(0, width, size):
        stop = start + size
        block = jnp.concatenate([work[start:stop, start:stop], eye], axis=1)
        small = eliminate(block, size)[:, size:]
        rows = lax.dot_general(
            small, work[start:stop, :], (((1,), (0,)), ((), ())),
            precision=lax.Precision.HIGHEST, preferred_element_type=jnp.float32,
        )
        work[start:stop, :] = rows
        if stop < width:
            work[stop:, :] -= lax.dot_general(
                rows[:, stop:width], rows, (((0,), (0,)), ((), ())),
                precision=lax.Precision.HIGHEST, preferred_element_type=jnp.float32,
            )
    lower[...] = jnp.where(row_of >= col_of, work[:, :width].T, 0.0)
    solved = work[:, width:]
    inverse[...] = solved
    panel_factor[...] = dot_last(
        split_three(panel[...], 1, False), split_three(solved, 1, True)
    )


def factor(whole_diag, panel):
    width = whole_diag.shape[0]
    square = jax.ShapeDtypeStruct((width, width), jnp.float32)
    return pl.pallas_call(
        factor_kernel,
        out_shape=(square, square, jax.ShapeDtypeStruct(panel.shape, jnp.float32)),
        in_specs=[pl.BlockSpec(memory_space=pltpu.VMEM)] * 2,
        out_specs=[pl.BlockSpec(memory_space=pltpu.VMEM)] * 3,
        scratch_shapes=[pltpu.VMEM((width, 2 * width), jnp.float32)],
        compiler_params=pltpu.CompilerParams(vmem_limit_bytes=24 * MIB),
        cost_estimate=pl.CostEstimate(
            flops=0, bytes_accessed=128 * MIB, transcendentals=0
        ),
        name="factor",
    )(whole_diag, panel)


def update_kernel(ratio, step_cols, row_raw, col_raw, inverse, trailing, out, right):
    width = inverse.shape[0]
    per_block = col_raw.shape[0] // (ratio * BLOCK)
    inverse_parts = split_three(inverse[...], 1, True)

    @pl.when(pl.program_id(0) == 0)
    def _():
        def one_block(m, carry):
            source = lax.rem(m, ratio) * per_block + m // ratio
            raw = col_raw[pl.ds(pl.multiple_of(source * BLOCK, BLOCK), BLOCK), :]
            factor_t = dot_last(inverse_parts, split_three(raw, 1, False))
            cols = pl.ds(pl.multiple_of(m * BLOCK, BLOCK), BLOCK)
            right[:, cols] = split_three(factor_t, 0, False)
            return carry

        lax.fori_loop(0, ratio * per_block, one_block, 0, unroll=2)

    left = split_three(dot_last(split_three(row_raw[...], 1, False), inverse_parts), 1, True)
    for start in range(0, trailing.shape[1], step_cols):
        cols = slice(start, start + step_cols)
        product = jnp.dot(left, right[:, cols], preferred_element_type=jnp.float32)
        out[:, cols] = (trailing[:, cols].astype(jnp.float32) - product).astype(jnp.bfloat16)


def largest(total, options):
    return next((o for o in options if total % o == 0), total)


def update(row_raw, col_raw, inverse, trailing, ratio):
    rows, cols = trailing.shape
    width = inverse.shape[0]
    tile = largest(rows, (512, 256))
    return pl.pallas_call(
        functools.partial(update_kernel, ratio, largest(cols, (512, 256))),
        grid=(rows // tile,),
        out_shape=jax.ShapeDtypeStruct((rows, cols), jnp.bfloat16),
        in_specs=[
            pl.BlockSpec((tile, width), lambda r: (r, 0)),
            pl.BlockSpec(memory_space=pltpu.VMEM),
            pl.BlockSpec(memory_space=pltpu.VMEM),
            pl.BlockSpec((tile, cols), lambda r: (r, 0)),
        ],
        out_specs=pl.BlockSpec((tile, cols), lambda r: (r, 0)),
        scratch_shapes=[pltpu.VMEM((3 * width, cols), jnp.bfloat16)],
        compiler_params=pltpu.CompilerParams(vmem_limit_bytes=56 * MIB),
        cost_estimate=pl.CostEstimate(
            flops=6 * rows * cols * width, bytes_accessed=4 * rows * cols, transcendentals=0
        ),
        name="update",
    )(row_raw, col_raw, inverse, trailing)


def per_device(diag_block, panel, trailing):
    n_row, n_col = lax.axis_size("row"), lax.axis_size("col")
    ratio = n_row // n_col
    swap = []
    for turn in range(ratio):
        for a in range(n_col):
            for b in range(n_col):
                source = (turn * n_col + a) * n_col + b
                swap.append((source, (turn * n_col + b) * n_col + a))
    column_share = lax.ppermute(panel, ("row", "col"), swap)
    column_raw = lax.all_gather(column_share, "row", axis=0, tiled=True)
    row_raw = lax.all_gather(panel, "col", axis=0, tiled=True)

    whole_diag = gather_diag(diag_block, n_row, n_col)
    lower, inverse, panel_factor = factor(whole_diag, panel)
    share = diag_block.shape[0]
    me = lax.axis_index(("row", "col"))
    factor_rows = lax.dynamic_slice_in_dim(lower, me * share, share, 0)
    trailing_out = update(row_raw, column_raw, inverse, trailing, ratio)
    return (factor_rows, panel_factor, trailing_out)


def solution(mesh):
    placed = (P(("row", "col"), None), P(("row", "col"), None), P("row", "col"))
    return jax.shard_map(
        per_device,
        mesh=mesh,
        in_specs=placed,
        out_specs=placed,
        check_vma=False,
    )
```

```python
import functools

import jax
import jax.numpy as jnp
import numpy as np
from jax import lax
from jax.experimental import pallas as pl
from jax.experimental.pallas import tpu as pltpu
from jax.sharding import PartitionSpec as P

BLOCK = 256
MIB = 1 << 20
MESH = pl.DeviceIdType.MESH


def split_three(x, axis, first):
    high = x.astype(jnp.bfloat16)
    low = (x - high.astype(jnp.float32)).astype(jnp.bfloat16)
    return jnp.concatenate([high, high, low] if first else [high, low, high], axis=axis)


def dot_last(a, b):
    return lax.dot_general(
        a, b, (((1,), (1,)), ((), ())), preferred_element_type=jnp.float32
    )


def gather_diag_kernel(n_row, n_col, mine, whole, held, send_sem, recv_sem):
    count = n_row * n_col
    me = lax.axis_index("row") * n_col + lax.axis_index("col")

    def target(step):
        other = lax.rem(me + step, count)
        return (other // n_col, lax.rem(other, n_col))

    barrier = pltpu.get_barrier_semaphore()

    def greet(step, carry):
        pl.semaphore_signal(barrier, inc=1, device_id=target(step), device_id_type=MESH)
        return carry

    lax.fori_loop(1, count, greet, 0)
    pl.semaphore_wait(barrier, count - 1)
    def send(step, carry):
        pltpu.make_async_remote_copy(
            src_ref=mine,
            dst_ref=held.at[me],
            send_sem=send_sem,
            recv_sem=recv_sem,
            device_id=target(step),
            device_id_type=MESH,
        ).start()
        return carry

    lax.fori_loop(1, count, send, 0)
    held[me] = mine[...]
    others = held.at[pl.ds(0, count - 1)]
    pltpu.make_async_copy(others, others, recv_sem).wait()
    pltpu.make_async_copy(others, others, send_sem).wait()
    whole[...] = held[...]


def gather_diag(diag_block, n_row, n_col):
    share, width = diag_block.shape
    whole = (n_row * n_col, share, width)
    gathered = pl.pallas_call(
        functools.partial(gather_diag_kernel, n_row, n_col),
        out_shape=jax.ShapeDtypeStruct(whole, jnp.float32),
        in_specs=[pl.BlockSpec(memory_space=pltpu.VMEM)],
        out_specs=pl.BlockSpec(memory_space=pltpu.VMEM),
        scratch_shapes=[
            pltpu.VMEM(whole, jnp.float32),
            pltpu.SemaphoreType.DMA,
            pltpu.SemaphoreType.DMA,
        ],
        compiler_params=pltpu.CompilerParams(collective_id=0, has_side_effects=True),
        cost_estimate=pl.CostEstimate(flops=0, bytes_accessed=16 * MIB, transcendentals=0),
        name="gather_diag",
    )(diag_block)
    return gathered.reshape(-1, width)


def eliminate(block, size):
    row_of = lax.broadcasted_iota(jnp.int32, (size, 2 * size), 0)
    col_of = lax.broadcasted_iota(jnp.int32, (size, 2 * size), 1)
    for j in range(size - 1):
        pivot_row = block[j : j + 1, :]
        scaled = pivot_row * (1.0 / block[j : j + 1, j : j + 1])
        factors = jnp.where(row_of > j, block[:, j : j + 1], 0.0)
        block = block - factors * scaled
    pivots = jnp.sum(jnp.where(row_of == col_of, block, 0.0), axis=1, keepdims=True)
    return block / jnp.sqrt(pivots)


def factor_kernel(diag, panel, lower, inverse, panel_factor, work):
    width = diag.shape[0]
    size = min(64, width)
    row_of = lax.broadcasted_iota(jnp.int32, (width, width), 0)
    col_of = lax.broadcasted_iota(jnp.int32, (width, width), 1)
    work[:, :width] = diag[...]
    work[:, width:] = jnp.where(row_of == col_of, 1.0, 0.0)
    eye = jnp.where(row_of == col_of, 1.0, 0.0)[:size, :size]
    for start in range(0, width, size):
        stop = start + size
        block = jnp.concatenate([work[start:stop, start:stop], eye], axis=1)
        small = eliminate(block, size)[:, size:]
        rows = lax.dot_general(
            small, work[start:stop, :], (((1,), (0,)), ((), ())),
            precision=lax.Precision.HIGHEST, preferred_element_type=jnp.float32,
        )
        work[start:stop, :] = rows
        if stop < width:
            work[stop:, :] -= lax.dot_general(
                rows[:, stop:width], rows, (((0,), (0,)), ((), ())),
                precision=lax.Precision.HIGHEST, preferred_element_type=jnp.float32,
            )
    lower[...] = jnp.where(row_of >= col_of, work[:, :width].T, 0.0)
    solved = work[:, width:]
    inverse[...] = solved
    panel_factor[...] = dot_last(
        split_three(panel[...], 1, False), split_three(solved, 1, True)
    )


def factor(whole_diag, panel):
    width = whole_diag.shape[0]
    square = jax.ShapeDtypeStruct((width, width), jnp.float32)
    return pl.pallas_call(
        factor_kernel,
        out_shape=(square, square, jax.ShapeDtypeStruct(panel.shape, jnp.float32)),
        in_specs=[pl.BlockSpec(memory_space=pltpu.VMEM)] * 2,
        out_specs=[pl.BlockSpec(memory_space=pltpu.VMEM)] * 3,
        scratch_shapes=[pltpu.VMEM((width, 2 * width), jnp.float32)],
        compiler_params=pltpu.CompilerParams(vmem_limit_bytes=24 * MIB),
        cost_estimate=pl.CostEstimate(
            flops=0, bytes_accessed=128 * MIB, transcendentals=0
        ),
        name="factor",
    )(whole_diag, panel)


def update_kernel(ratio, step_cols, row_raw, col_raw, inverse, trailing, out, right):
    width = inverse.shape[0]
    per_block = col_raw.shape[0] // (ratio * BLOCK)
    inverse_parts = split_three(inverse[...], 1, True)

    @pl.when(pl.program_id(0) == 0)
    def _():
        def one_block(m, carry):
            source = lax.rem(m, ratio) * per_block + m // ratio
            raw = col_raw[pl.ds(pl.multiple_of(source * BLOCK, BLOCK), BLOCK), :]
            factor_t = dot_last(inverse_parts, split_three(raw, 1, False))
            cols = pl.ds(pl.multiple_of(m * BLOCK, BLOCK), BLOCK)
            right[:, cols] = split_three(factor_t, 0, False)
            return carry

        lax.fori_loop(0, ratio * per_block, one_block, 0, unroll=2)

    left = split_three(dot_last(split_three(row_raw[...], 1, False), inverse_parts), 1, True)
    for start in range(0, trailing.shape[1], step_cols):
        cols = slice(start, start + step_cols)
        product = jnp.dot(left, right[:, cols], preferred_element_type=jnp.float32)
        out[:, cols] = (trailing[:, cols].astype(jnp.float32) - product).astype(jnp.bfloat16)


def largest(total, options):
    return next((o for o in options if total % o == 0), total)


def update(row_raw, col_raw, inverse, trailing, ratio):
    rows, cols = trailing.shape
    width = inverse.shape[0]
    tile = largest(rows, (512, 256))
    return pl.pallas_call(
        functools.partial(update_kernel, ratio, largest(cols, (512, 256))),
        grid=(rows // tile,),
        out_shape=jax.ShapeDtypeStruct((rows, cols), jnp.bfloat16),
        in_specs=[
            pl.BlockSpec((tile, width), lambda r: (r, 0)),
            pl.BlockSpec(memory_space=pltpu.VMEM),
            pl.BlockSpec(memory_space=pltpu.VMEM),
            pl.BlockSpec((tile, cols), lambda r: (r, 0)),
        ],
        out_specs=pl.BlockSpec((tile, cols), lambda r: (r, 0)),
        scratch_shapes=[pltpu.VMEM((3 * width, cols), jnp.bfloat16)],
        compiler_params=pltpu.CompilerParams(vmem_limit_bytes=56 * MIB),
        cost_estimate=pl.CostEstimate(
            flops=6 * rows * cols * width, bytes_accessed=4 * rows * cols, transcendentals=0
        ),
        name="update",
    )(row_raw, col_raw, inverse, trailing)


def left_kernel(row_raw, inverse, left):
    inverse_parts = split_three(inverse[...], 1, True)
    left[...] = split_three(
        dot_last(split_three(row_raw[...], 1, False), inverse_parts), 1, True
    )


def make_left(row_raw, inverse):
    rows, width = row_raw.shape
    tile = largest(rows, (768, 512, 256))
    return pl.pallas_call(
        left_kernel,
        grid=(rows // tile,),
        out_shape=jax.ShapeDtypeStruct((rows, 3 * width), jnp.bfloat16),
        in_specs=[
            pl.BlockSpec((tile, width), lambda r: (r, 0)),
            pl.BlockSpec((width, width), lambda r: (0, 0)),
        ],
        out_specs=pl.BlockSpec((tile, 3 * width), lambda r: (r, 0)),
        compiler_params=pltpu.CompilerParams(vmem_limit_bytes=24 * MIB),
        cost_estimate=pl.CostEstimate(
            flops=6 * rows * width * width, bytes_accessed=10 * rows * width, transcendentals=0
        ),
        name="left",
    )(row_raw, inverse)


def strips_kernel(shares, per_share, step_rows, *refs):
    raws = refs[1 : 1 + shares]
    left, inverse, trailing = refs[1 + shares : 4 + shares]
    out, right = refs[-2:]
    step = pl.program_id(0)
    inverse_parts = split_three(inverse[...], 1, True)
    for number, raw in enumerate(raws):

        @pl.when(step // per_share == number)
        def _():
            first = pl.multiple_of((step - number * per_share) * BLOCK, BLOCK)
            rows = raw[pl.ds(first, BLOCK), :]
            right[...] = split_three(
                dot_last(inverse_parts, split_three(rows, 1, False)), 0, False
            )

    for start in range(0, trailing.shape[0], step_rows):
        rows = slice(start, start + step_rows)
        product = jnp.dot(left[rows, :], right[...], preferred_element_type=jnp.float32)
        out[rows, :] = (trailing[rows, :].astype(jnp.float32) - product).astype(jnp.bfloat16)


def update_strips(columns, raws, left, inverse, trailing, out):
    rows = trailing.shape[0]
    width = inverse.shape[0]
    per_share = raws[0].shape[0] // BLOCK
    steps = len(raws) * per_share
    strip = pl.BlockSpec((rows, BLOCK), lambda k, columns: (0, columns[k]))
    whole = pl.BlockSpec(memory_space=pltpu.VMEM)
    operands = [columns, *raws, left, inverse, trailing]
    in_specs = [whole] * (len(raws) + 2) + [strip]
    aliases = {}
    if out is not None:
        aliases = {len(operands): 0}
        operands.append(out)
        in_specs.append(pl.BlockSpec(memory_space=pl.ANY))
    return pl.pallas_call(
        functools.partial(strips_kernel, len(raws), per_share, largest(rows, (512, 256))),
        grid_spec=pltpu.PrefetchScalarGridSpec(
            num_scalar_prefetch=1,
            grid=(steps,),
            in_specs=in_specs,
            out_specs=strip,
            scratch_shapes=[pltpu.VMEM((3 * width, BLOCK), jnp.bfloat16)],
        ),
        out_shape=jax.ShapeDtypeStruct(trailing.shape, jnp.bfloat16),
        input_output_aliases=aliases,
        compiler_params=pltpu.CompilerParams(vmem_limit_bytes=32 * MIB),
        cost_estimate=pl.CostEstimate(
            flops=6 * rows * steps * BLOCK * width,
            bytes_accessed=4 * rows * steps * BLOCK,
            transcendentals=0,
        ),
        name="strips",
    )(*operands)


def ring_tables(n_row, n_col, per_share):
    ring = list(range(0, n_row, 2)) + list(range(n_row - 1, 0, -2))
    table = np.zeros((n_row, n_row, per_share), np.int32)
    for place, row in enumerate(ring):
        for distance in range(n_row):
            turn, share = divmod(ring[(place - distance) % n_row], n_col)
            for q in range(per_share):
                table[row, distance, q] = (share * per_share + q) * (n_row // n_col) + turn
    forward = [(ring[p], ring[(p + 1) % n_row]) for p in range(n_row)]
    return forward, [(b, a) for a, b in forward], table


def ring_update(share, whole_diag, panel, trailing):
    n_row, n_col = lax.axis_size("row"), lax.axis_size("col")
    per_share = share.shape[0] // BLOCK
    forward, backward, table = ring_tables(n_row, n_col, per_share)
    columns = lax.dynamic_index_in_dim(
        jnp.asarray(table), lax.axis_index("row"), 0, keepdims=False
    )
    row_raw = lax.all_gather(panel, "col", axis=0, tiled=True)
    ahead = lax.ppermute(share, "row", forward)
    behind = lax.ppermute(share, "row", backward)
    lower, inverse, panel_factor = factor(whole_diag, panel)
    ahead, behind, inverse = lax.optimization_barrier((ahead, behind, inverse))
    left = make_left(row_raw, inverse)
    out, ready, numbers = None, [share], [0]
    middle, half = n_row // 2, share.shape[0] // 2
    for distance in range(1, middle + 1):
        ready, numbers = ready + [ahead, behind], numbers + [distance, n_row - distance]
        if distance < middle - 1:
            ahead = lax.ppermute(ahead, "row", forward)
            behind = lax.ppermute(behind, "row", backward)
        elif distance == middle - 1:
            ahead = lax.ppermute(ahead[:half], "row", forward)
            behind = lax.ppermute(behind[half:], "row", backward)
        else:
            ready, numbers = [jnp.concatenate([ahead, behind])], [middle]
        wanted = jnp.concatenate([columns[number] for number in numbers])
        out = update_strips(wanted, ready, left, inverse, trailing, out)
        if distance < middle:
            ahead, behind, out = lax.optimization_barrier((ahead, behind, out))
        ready, numbers = [], []
    return lower, panel_factor, out


def per_device(diag_block, panel, trailing):
    n_row, n_col = lax.axis_size("row"), lax.axis_size("col")
    ratio = n_row // n_col
    swap = []
    for turn in range(ratio):
        for a in range(n_col):
            for b in range(n_col):
                source = (turn * n_col + a) * n_col + b
                swap.append((source, (turn * n_col + b) * n_col + a))
    column_share = lax.ppermute(panel, ("row", "col"), swap)
    whole_diag = gather_diag(diag_block, n_row, n_col)
    if panel.shape[0] % BLOCK == 0 and n_row % 2 == 0 and n_row >= 4:
        column_share, whole_diag = lax.optimization_barrier((column_share, whole_diag))
        lower, panel_factor, trailing_out = ring_update(
            column_share, whole_diag, panel, trailing
        )
    else:
        column_raw = lax.all_gather(column_share, "row", axis=0, tiled=True)
        row_raw = lax.all_gather(panel, "col", axis=0, tiled=True)
        lower, inverse, panel_factor = factor(whole_diag, panel)
        trailing_out = update(row_raw, column_raw, inverse, trailing, ratio)
    share = diag_block.shape[0]
    me = lax.axis_index(("row", "col"))
    factor_rows = lax.dynamic_slice_in_dim(lower, me * share, share, 0)
    return (factor_rows, panel_factor, trailing_out)


def solution(mesh):
    placed = (P(("row", "col"), None), P(("row", "col"), None), P("row", "col"))
    return jax.shard_map(
        per_device,
        mesh=mesh,
        in_specs=placed,
        out_specs=placed,
        check_vma=False,
    )
```

```python
import functools

import jax
import jax.numpy as jnp
import numpy as np
from jax import lax
from jax.experimental import pallas as pl
from jax.experimental.pallas import tpu as pltpu
from jax.sharding import PartitionSpec as P

BLOCK = 256
MIB = 1 << 20
MESH = pl.DeviceIdType.MESH


def split_three(x, axis, first):
    high = x.astype(jnp.bfloat16)
    low = (x - high.astype(jnp.float32)).astype(jnp.bfloat16)
    return jnp.concatenate([high, high, low] if first else [high, low, high], axis=axis)


def dot_last(a, b):
    return lax.dot_general(
        a, b, (((1,), (1,)), ((), ())), preferred_element_type=jnp.float32
    )


def gather_diag_kernel(n_row, n_col, mine, whole, held, send_sem, recv_sem):
    count = n_row * n_col
    me = lax.axis_index("row") * n_col + lax.axis_index("col")

    def target(step):
        other = lax.rem(me + step, count)
        return (other // n_col, lax.rem(other, n_col))

    barrier = pltpu.get_barrier_semaphore()

    def greet(step, carry):
        pl.semaphore_signal(barrier, inc=1, device_id=target(step), device_id_type=MESH)
        return carry

    lax.fori_loop(1, count, greet, 0)
    pl.semaphore_wait(barrier, count - 1)
    def send(step, carry):
        pltpu.make_async_remote_copy(
            src_ref=mine,
            dst_ref=held.at[me],
            send_sem=send_sem,
            recv_sem=recv_sem,
            device_id=target(step),
            device_id_type=MESH,
        ).start()
        return carry

    lax.fori_loop(1, count, send, 0)
    held[me] = mine[...]
    others = held.at[pl.ds(0, count - 1)]
    pltpu.make_async_copy(others, others, recv_sem).wait()
    pltpu.make_async_copy(others, others, send_sem).wait()
    whole[...] = held[...]


def gather_diag(diag_block, n_row, n_col):
    share, width = diag_block.shape
    whole = (n_row * n_col, share, width)
    gathered = pl.pallas_call(
        functools.partial(gather_diag_kernel, n_row, n_col),
        out_shape=jax.ShapeDtypeStruct(whole, jnp.float32),
        in_specs=[pl.BlockSpec(memory_space=pltpu.VMEM)],
        out_specs=pl.BlockSpec(memory_space=pltpu.VMEM),
        scratch_shapes=[
            pltpu.VMEM(whole, jnp.float32),
            pltpu.SemaphoreType.DMA,
            pltpu.SemaphoreType.DMA,
        ],
        compiler_params=pltpu.CompilerParams(collective_id=0, has_side_effects=True),
        cost_estimate=pl.CostEstimate(flops=0, bytes_accessed=16 * MIB, transcendentals=0),
        name="gather_diag",
    )(diag_block)
    return gathered.reshape(-1, width)


def eliminate(block, size):
    row_of = lax.broadcasted_iota(jnp.int32, (size, 2 * size), 0)
    col_of = lax.broadcasted_iota(jnp.int32, (size, 2 * size), 1)
    for j in range(size - 1):
        pivot_row = block[j : j + 1, :]
        scaled = pivot_row * (1.0 / block[j : j + 1, j : j + 1])
        factors = jnp.where(row_of > j, block[:, j : j + 1], 0.0)
        block = block - factors * scaled
    pivots = jnp.sum(jnp.where(row_of == col_of, block, 0.0), axis=1, keepdims=True)
    return block / jnp.sqrt(pivots)


def factor_kernel(diag, panel, lower, inverse, panel_factor, work):
    width = diag.shape[0]
    size = min(64, width)
    row_of = lax.broadcasted_iota(jnp.int32, (width, width), 0)
    col_of = lax.broadcasted_iota(jnp.int32, (width, width), 1)
    work[:, :width] = diag[...]
    work[:, width:] = jnp.where(row_of == col_of, 1.0, 0.0)
    eye = jnp.where(row_of == col_of, 1.0, 0.0)[:size, :size]
    for start in range(0, width, size):
        stop = start + size
        block = jnp.concatenate([work[start:stop, start:stop], eye], axis=1)
        small = eliminate(block, size)[:, size:]
        rows = lax.dot_general(
            small, work[start:stop, :], (((1,), (0,)), ((), ())),
            precision=lax.Precision.HIGHEST, preferred_element_type=jnp.float32,
        )
        work[start:stop, :] = rows
        if stop < width:
            work[stop:, :] -= lax.dot_general(
                rows[:, stop:width], rows, (((0,), (0,)), ((), ())),
                precision=lax.Precision.HIGHEST, preferred_element_type=jnp.float32,
            )
    lower[...] = jnp.where(row_of >= col_of, work[:, :width].T, 0.0)
    solved = work[:, width:]
    inverse[...] = solved
    panel_factor[...] = dot_last(
        split_three(panel[...], 1, False), split_three(solved, 1, True)
    )


def factor(whole_diag, panel):
    width = whole_diag.shape[0]
    square = jax.ShapeDtypeStruct((width, width), jnp.float32)
    return pl.pallas_call(
        factor_kernel,
        out_shape=(square, square, jax.ShapeDtypeStruct(panel.shape, jnp.float32)),
        in_specs=[pl.BlockSpec(memory_space=pltpu.VMEM)] * 2,
        out_specs=[pl.BlockSpec(memory_space=pltpu.VMEM)] * 3,
        scratch_shapes=[pltpu.VMEM((width, 2 * width), jnp.float32)],
        compiler_params=pltpu.CompilerParams(vmem_limit_bytes=24 * MIB),
        cost_estimate=pl.CostEstimate(
            flops=0, bytes_accessed=128 * MIB, transcendentals=0
        ),
        name="factor",
    )(whole_diag, panel)


def update_kernel(ratio, step_cols, row_raw, col_raw, inverse, trailing, out, right):
    width = inverse.shape[0]
    per_block = col_raw.shape[0] // (ratio * BLOCK)
    inverse_parts = split_three(inverse[...], 1, True)

    @pl.when(pl.program_id(0) == 0)
    def _():
        def one_block(m, carry):
            source = lax.rem(m, ratio) * per_block + m // ratio
            raw = col_raw[pl.ds(pl.multiple_of(source * BLOCK, BLOCK), BLOCK), :]
            factor_t = dot_last(inverse_parts, split_three(raw, 1, False))
            cols = pl.ds(pl.multiple_of(m * BLOCK, BLOCK), BLOCK)
            right[:, cols] = split_three(factor_t, 0, False)
            return carry

        lax.fori_loop(0, ratio * per_block, one_block, 0, unroll=2)

    left = split_three(dot_last(split_three(row_raw[...], 1, False), inverse_parts), 1, True)
    for start in range(0, trailing.shape[1], step_cols):
        cols = slice(start, start + step_cols)
        product = jnp.dot(left, right[:, cols], preferred_element_type=jnp.float32)
        out[:, cols] = (trailing[:, cols].astype(jnp.float32) - product).astype(jnp.bfloat16)


def largest(total, options):
    return next((o for o in options if total % o == 0), total)


def update(row_raw, col_raw, inverse, trailing, ratio):
    rows, cols = trailing.shape
    width = inverse.shape[0]
    tile = largest(rows, (512, 256))
    return pl.pallas_call(
        functools.partial(update_kernel, ratio, largest(cols, (512, 256))),
        grid=(rows // tile,),
        out_shape=jax.ShapeDtypeStruct((rows, cols), jnp.bfloat16),
        in_specs=[
            pl.BlockSpec((tile, width), lambda r: (r, 0)),
            pl.BlockSpec(memory_space=pltpu.VMEM),
            pl.BlockSpec(memory_space=pltpu.VMEM),
            pl.BlockSpec((tile, cols), lambda r: (r, 0)),
        ],
        out_specs=pl.BlockSpec((tile, cols), lambda r: (r, 0)),
        scratch_shapes=[pltpu.VMEM((3 * width, cols), jnp.bfloat16)],
        compiler_params=pltpu.CompilerParams(vmem_limit_bytes=56 * MIB),
        cost_estimate=pl.CostEstimate(
            flops=6 * rows * cols * width, bytes_accessed=4 * rows * cols, transcendentals=0
        ),
        name="update",
    )(row_raw, col_raw, inverse, trailing)


def left_kernel(row_raw, inverse, left):
    inverse_parts = split_three(inverse[...], 1, True)
    left[...] = split_three(
        dot_last(split_three(row_raw[...], 1, False), inverse_parts), 1, True
    )


def make_left(row_raw, inverse):
    rows, width = row_raw.shape
    tile = largest(rows, (768, 512, 256))
    return pl.pallas_call(
        left_kernel,
        grid=(rows // tile,),
        out_shape=jax.ShapeDtypeStruct((rows, 3 * width), jnp.bfloat16),
        in_specs=[
            pl.BlockSpec((tile, width), lambda r: (r, 0)),
            pl.BlockSpec((width, width), lambda r: (0, 0)),
        ],
        out_specs=pl.BlockSpec((tile, 3 * width), lambda r: (r, 0)),
        compiler_params=pltpu.CompilerParams(vmem_limit_bytes=24 * MIB),
        cost_estimate=pl.CostEstimate(
            flops=6 * rows * width * width, bytes_accessed=10 * rows * width, transcendentals=0
        ),
        name="left",
    )(row_raw, inverse)


def strips_kernel(shares, per_share, step_rows, *refs):
    raws = refs[1 : 1 + shares]
    left, inverse, trailing = refs[1 + shares : 4 + shares]
    out, right = refs[-2:]
    step = pl.program_id(0)
    inverse_parts = split_three(inverse[...], 1, True)
    for number, raw in enumerate(raws):

        @pl.when(step // per_share == number)
        def _():
            first = pl.multiple_of((step - number * per_share) * BLOCK, BLOCK)
            rows = raw[pl.ds(first, BLOCK), :]
            right[...] = split_three(
                dot_last(inverse_parts, split_three(rows, 1, False)), 0, False
            )

    for start in range(0, trailing.shape[0], step_rows):
        rows = slice(start, start + step_rows)
        product = jnp.dot(left[rows, :], right[...], preferred_element_type=jnp.float32)
        out[rows, :] = (trailing[rows, :].astype(jnp.float32) - product).astype(jnp.bfloat16)


def update_strips(columns, raws, left, inverse, trailing, out):
    rows = trailing.shape[0]
    width = inverse.shape[0]
    per_share = raws[0].shape[0] // BLOCK
    steps = len(raws) * per_share
    strip = pl.BlockSpec((rows, BLOCK), lambda k, columns: (0, columns[k]))
    whole = pl.BlockSpec(memory_space=pltpu.VMEM)
    operands = [columns, *raws, left, inverse, trailing]
    in_specs = [whole] * (len(raws) + 2) + [strip]
    aliases = {}
    if out is not None:
        aliases = {len(operands): 0}
        operands.append(out)
        in_specs.append(pl.BlockSpec(memory_space=pl.ANY))
    return pl.pallas_call(
        functools.partial(strips_kernel, len(raws), per_share, rows),
        grid_spec=pltpu.PrefetchScalarGridSpec(
            num_scalar_prefetch=1,
            grid=(steps,),
            in_specs=in_specs,
            out_specs=strip,
            scratch_shapes=[pltpu.VMEM((3 * width, BLOCK), jnp.bfloat16)],
        ),
        out_shape=jax.ShapeDtypeStruct(trailing.shape, jnp.bfloat16),
        input_output_aliases=aliases,
        compiler_params=pltpu.CompilerParams(vmem_limit_bytes=40 * MIB),
        cost_estimate=pl.CostEstimate(
            flops=6 * rows * steps * BLOCK * width,
            bytes_accessed=4 * rows * steps * BLOCK,
            transcendentals=0,
        ),
        name="strips",
    )(*operands)


def ring_tables(n_row, n_col, per_share):
    ring = list(range(0, n_row, 2)) + list(range(n_row - 1, 0, -2))
    table = np.zeros((n_row, n_row, per_share), np.int32)
    for place, row in enumerate(ring):
        for distance in range(n_row):
            turn, share = divmod(ring[(place - distance) % n_row], n_col)
            for q in range(per_share):
                table[row, distance, q] = (share * per_share + q) * (n_row // n_col) + turn
    forward = [(ring[p], ring[(p + 1) % n_row]) for p in range(n_row)]
    return forward, [(b, a) for a, b in forward], table


def ring_update(share, whole_diag, panel, trailing):
    n_row, n_col = lax.axis_size("row"), lax.axis_size("col")
    per_share = share.shape[0] // BLOCK
    forward, backward, table = ring_tables(n_row, n_col, per_share)
    columns = lax.dynamic_index_in_dim(
        jnp.asarray(table), lax.axis_index("row"), 0, keepdims=False
    )
    row_raw = lax.all_gather(panel, "col", axis=0, tiled=True)
    lower, inverse, panel_factor = factor(whole_diag, panel)
    share, inverse = lax.optimization_barrier((share, inverse))
    ahead = lax.ppermute(share, "row", forward)
    behind = lax.ppermute(share, "row", backward)
    left = make_left(row_raw, inverse)
    ahead, behind, left = lax.optimization_barrier((ahead, behind, left))
    out, ready, numbers = None, [share], [0]
    middle, half = n_row // 2, share.shape[0] // 2
    for distance in range(1, middle + 1):
        ready, numbers = ready + [ahead, behind], numbers + [distance, n_row - distance]
        if distance < middle - 1:
            ahead = lax.ppermute(ahead, "row", forward)
            behind = lax.ppermute(behind, "row", backward)
        elif distance == middle - 1:
            ahead = lax.ppermute(ahead[:half], "row", forward)
            behind = lax.ppermute(behind[half:], "row", backward)
        else:
            ready, numbers = [jnp.concatenate([ahead, behind])], [middle]
        wanted = jnp.concatenate([columns[number] for number in numbers])
        out = update_strips(wanted, ready, left, inverse, trailing, out)
        if distance < middle:
            ahead, behind, out = lax.optimization_barrier((ahead, behind, out))
        ready, numbers = [], []
    return lower, panel_factor, out


def per_device(diag_block, panel, trailing):
    n_row, n_col = lax.axis_size("row"), lax.axis_size("col")
    ratio = n_row // n_col
    swap = []
    for turn in range(ratio):
        for a in range(n_col):
            for b in range(n_col):
                source = (turn * n_col + a) * n_col + b
                swap.append((source, (turn * n_col + b) * n_col + a))
    whole_diag = gather_diag(diag_block, n_row, n_col)
    panel, whole_diag = lax.optimization_barrier((panel, whole_diag))
    column_share = lax.ppermute(panel, ("row", "col"), swap)
    if panel.shape[0] % BLOCK == 0 and n_row % 2 == 0 and n_row >= 4:
        lower, panel_factor, trailing_out = ring_update(
            column_share, whole_diag, panel, trailing
        )
    else:
        column_raw = lax.all_gather(column_share, "row", axis=0, tiled=True)
        row_raw = lax.all_gather(panel, "col", axis=0, tiled=True)
        lower, inverse, panel_factor = factor(whole_diag, panel)
        trailing_out = update(row_raw, column_raw, inverse, trailing, ratio)
    share = diag_block.shape[0]
    me = lax.axis_index(("row", "col"))
    factor_rows = lax.dynamic_slice_in_dim(lower, me * share, share, 0)
    return (factor_rows, panel_factor, trailing_out)


def solution(mesh):
    placed = (P(("row", "col"), None), P(("row", "col"), None), P("row", "col"))
    return jax.shard_map(
        per_device,
        mesh=mesh,
        in_specs=placed,
        out_specs=placed,
        check_vma=False,
    )
```

```python
import functools

import jax
import jax.numpy as jnp
import numpy as np
from jax import lax
from jax.experimental import pallas as pl
from jax.experimental.pallas import tpu as pltpu
from jax.sharding import PartitionSpec as P

BLOCK = 256
MIB = 1 << 20
MESH = pl.DeviceIdType.MESH


def split_three(x, axis, first):
    high = x.astype(jnp.bfloat16)
    low = (x - high.astype(jnp.float32)).astype(jnp.bfloat16)
    return jnp.concatenate([high, high, low] if first else [high, low, high], axis=axis)


def dot_last(a, b):
    return lax.dot_general(
        a, b, (((1,), (1,)), ((), ())), preferred_element_type=jnp.float32
    )


def gather_diag_kernel(n_row, n_col, mine, whole, held, send_sem, recv_sem):
    count = n_row * n_col
    me = lax.axis_index("row") * n_col + lax.axis_index("col")

    def target(step):
        other = lax.rem(me + step, count)
        return (other // n_col, lax.rem(other, n_col))

    barrier = pltpu.get_barrier_semaphore()

    def greet(step, carry):
        pl.semaphore_signal(barrier, inc=1, device_id=target(step), device_id_type=MESH)
        return carry

    lax.fori_loop(1, count, greet, 0)
    pl.semaphore_wait(barrier, count - 1)
    def send(step, carry):
        pltpu.make_async_remote_copy(
            src_ref=mine,
            dst_ref=held.at[me],
            send_sem=send_sem,
            recv_sem=recv_sem,
            device_id=target(step),
            device_id_type=MESH,
        ).start()
        return carry

    lax.fori_loop(1, count, send, 0)
    held[me] = mine[...]
    others = held.at[pl.ds(0, count - 1)]
    pltpu.make_async_copy(others, others, recv_sem).wait()
    pltpu.make_async_copy(others, others, send_sem).wait()
    whole[...] = held[...]


def gather_diag(diag_block, n_row, n_col):
    share, width = diag_block.shape
    whole = (n_row * n_col, share, width)
    gathered = pl.pallas_call(
        functools.partial(gather_diag_kernel, n_row, n_col),
        out_shape=jax.ShapeDtypeStruct(whole, jnp.float32),
        in_specs=[pl.BlockSpec(memory_space=pltpu.VMEM)],
        out_specs=pl.BlockSpec(memory_space=pltpu.VMEM),
        scratch_shapes=[
            pltpu.VMEM(whole, jnp.float32),
            pltpu.SemaphoreType.DMA,
            pltpu.SemaphoreType.DMA,
        ],
        compiler_params=pltpu.CompilerParams(collective_id=0, has_side_effects=True),
        cost_estimate=pl.CostEstimate(flops=0, bytes_accessed=16 * MIB, transcendentals=0),
        name="gather_diag",
    )(diag_block)
    return gathered.reshape(-1, width)


def eliminate(block, size):
    row_of = lax.broadcasted_iota(jnp.int32, (size, 2 * size), 0)
    col_of = lax.broadcasted_iota(jnp.int32, (size, 2 * size), 1)
    for j in range(size - 1):
        pivot_row = block[j : j + 1, :]
        scaled = pivot_row * (1.0 / block[j : j + 1, j : j + 1])
        factors = jnp.where(row_of > j, block[:, j : j + 1], 0.0)
        block = block - factors * scaled
    pivots = jnp.sum(jnp.where(row_of == col_of, block, 0.0), axis=1, keepdims=True)
    return block / jnp.sqrt(pivots)


def factor_kernel(diag, panel, lower, inverse, panel_factor, work):
    width = diag.shape[0]
    size = min(64, width)
    row_of = lax.broadcasted_iota(jnp.int32, (width, width), 0)
    col_of = lax.broadcasted_iota(jnp.int32, (width, width), 1)
    work[:, :width] = diag[...]
    work[:, width:] = jnp.where(row_of == col_of, 1.0, 0.0)
    eye = jnp.where(row_of == col_of, 1.0, 0.0)[:size, :size]
    for start in range(0, width, size):
        stop = start + size
        block = jnp.concatenate([work[start:stop, start:stop], eye], axis=1)
        small = eliminate(block, size)[:, size:]
        rows = lax.dot_general(
            small, work[start:stop, :], (((1,), (0,)), ((), ())),
            precision=lax.Precision.HIGHEST, preferred_element_type=jnp.float32,
        )
        work[start:stop, :] = rows
        if stop < width:
            work[stop:, :] -= lax.dot_general(
                rows[:, stop:width], rows, (((0,), (0,)), ((), ())),
                precision=lax.Precision.HIGHEST, preferred_element_type=jnp.float32,
            )
    lower[...] = jnp.where(row_of >= col_of, work[:, :width].T, 0.0)
    solved = work[:, width:]
    inverse[...] = solved
    panel_factor[...] = dot_last(
        split_three(panel[...], 1, False), split_three(solved, 1, True)
    )


def factor(whole_diag, panel):
    width = whole_diag.shape[0]
    square = jax.ShapeDtypeStruct((width, width), jnp.float32)
    return pl.pallas_call(
        factor_kernel,
        out_shape=(square, square, jax.ShapeDtypeStruct(panel.shape, jnp.float32)),
        in_specs=[pl.BlockSpec(memory_space=pltpu.VMEM)] * 2,
        out_specs=[pl.BlockSpec(memory_space=pltpu.VMEM)] * 3,
        scratch_shapes=[pltpu.VMEM((width, 2 * width), jnp.float32)],
        compiler_params=pltpu.CompilerParams(vmem_limit_bytes=24 * MIB),
        cost_estimate=pl.CostEstimate(
            flops=0, bytes_accessed=128 * MIB, transcendentals=0
        ),
        name="factor",
    )(whole_diag, panel)


def update_kernel(ratio, step_cols, row_raw, col_raw, inverse, trailing, out, right):
    width = inverse.shape[0]
    per_block = col_raw.shape[0] // (ratio * BLOCK)
    inverse_parts = split_three(inverse[...], 1, True)

    @pl.when(pl.program_id(0) == 0)
    def _():
        def one_block(m, carry):
            source = lax.rem(m, ratio) * per_block + m // ratio
            raw = col_raw[pl.ds(pl.multiple_of(source * BLOCK, BLOCK), BLOCK), :]
            factor_t = dot_last(inverse_parts, split_three(raw, 1, False))
            cols = pl.ds(pl.multiple_of(m * BLOCK, BLOCK), BLOCK)
            right[:, cols] = split_three(factor_t, 0, False)
            return carry

        lax.fori_loop(0, ratio * per_block, one_block, 0, unroll=2)

    left = split_three(dot_last(split_three(row_raw[...], 1, False), inverse_parts), 1, True)
    for start in range(0, trailing.shape[1], step_cols):
        cols = slice(start, start + step_cols)
        product = jnp.dot(left, right[:, cols], preferred_element_type=jnp.float32)
        out[:, cols] = (trailing[:, cols].astype(jnp.float32) - product).astype(jnp.bfloat16)


def largest(total, options):
    return next((o for o in options if total % o == 0), total)


def update(row_raw, col_raw, inverse, trailing, ratio):
    rows, cols = trailing.shape
    width = inverse.shape[0]
    tile = largest(rows, (512, 256))
    return pl.pallas_call(
        functools.partial(update_kernel, ratio, largest(cols, (512, 256))),
        grid=(rows // tile,),
        out_shape=jax.ShapeDtypeStruct((rows, cols), jnp.bfloat16),
        in_specs=[
            pl.BlockSpec((tile, width), lambda r: (r, 0)),
            pl.BlockSpec(memory_space=pltpu.VMEM),
            pl.BlockSpec(memory_space=pltpu.VMEM),
            pl.BlockSpec((tile, cols), lambda r: (r, 0)),
        ],
        out_specs=pl.BlockSpec((tile, cols), lambda r: (r, 0)),
        scratch_shapes=[pltpu.VMEM((3 * width, cols), jnp.bfloat16)],
        compiler_params=pltpu.CompilerParams(vmem_limit_bytes=56 * MIB),
        cost_estimate=pl.CostEstimate(
            flops=6 * rows * cols * width, bytes_accessed=4 * rows * cols, transcendentals=0
        ),
        name="update",
    )(row_raw, col_raw, inverse, trailing)


def left_kernel(row_raw, inverse, left):
    inverse_parts = split_three(inverse[...], 1, True)
    left[...] = split_three(
        dot_last(split_three(row_raw[...], 1, False), inverse_parts), 1, True
    )


def make_left(row_raw, inverse):
    rows, width = row_raw.shape
    tile = largest(rows, (768, 512, 256))
    return pl.pallas_call(
        left_kernel,
        grid=(rows // tile,),
        out_shape=jax.ShapeDtypeStruct((rows, 3 * width), jnp.bfloat16),
        in_specs=[
            pl.BlockSpec((tile, width), lambda r: (r, 0)),
            pl.BlockSpec((width, width), lambda r: (0, 0)),
        ],
        out_specs=pl.BlockSpec((tile, 3 * width), lambda r: (r, 0)),
        compiler_params=pltpu.CompilerParams(vmem_limit_bytes=24 * MIB),
        cost_estimate=pl.CostEstimate(
            flops=6 * rows * width * width, bytes_accessed=10 * rows * width, transcendentals=0
        ),
        name="left",
    )(row_raw, inverse)


def strips_kernel(shares, per_share, step_rows, *refs):
    raws = refs[1 : 1 + shares]
    left, inverse, trailing = refs[1 + shares : 4 + shares]
    out, right = refs[-2:]
    step = pl.program_id(0)
    inverse_parts = split_three(inverse[...], 1, True)
    for number, raw in enumerate(raws):

        @pl.when(step // per_share == number)
        def _():
            first = pl.multiple_of((step - number * per_share) * BLOCK, BLOCK)
            rows = raw[pl.ds(first, BLOCK), :]
            right[...] = split_three(
                dot_last(inverse_parts, split_three(rows, 1, False)), 0, False
            )

    for start in range(0, trailing.shape[0], step_rows):
        rows = slice(start, start + step_rows)
        product = jnp.dot(left[rows, :], right[...], preferred_element_type=jnp.float32)
        out[rows, :] = (trailing[rows, :].astype(jnp.float32) - product).astype(jnp.bfloat16)


def update_strips(columns, raws, left, inverse, trailing, out):
    rows = trailing.shape[0]
    width = inverse.shape[0]
    per_share = raws[0].shape[0] // BLOCK
    steps = len(raws) * per_share
    strip = pl.BlockSpec((rows, BLOCK), lambda k, columns: (0, columns[k]))
    whole = pl.BlockSpec(memory_space=pltpu.VMEM)
    operands = [columns, *raws, left, inverse, trailing]
    in_specs = [whole] * (len(raws) + 2) + [strip]
    aliases = {}
    if out is not None:
        aliases = {len(operands): 0}
        operands.append(out)
        in_specs.append(pl.BlockSpec(memory_space=pl.ANY))
    return pl.pallas_call(
        functools.partial(strips_kernel, len(raws), per_share, rows),
        grid_spec=pltpu.PrefetchScalarGridSpec(
            num_scalar_prefetch=1,
            grid=(steps,),
            in_specs=in_specs,
            out_specs=strip,
            scratch_shapes=[pltpu.VMEM((3 * width, BLOCK), jnp.bfloat16)],
        ),
        out_shape=jax.ShapeDtypeStruct(trailing.shape, jnp.bfloat16),
        input_output_aliases=aliases,
        compiler_params=pltpu.CompilerParams(vmem_limit_bytes=40 * MIB),
        cost_estimate=pl.CostEstimate(
            flops=6 * rows * steps * BLOCK * width,
            bytes_accessed=4 * rows * steps * BLOCK,
            transcendentals=0,
        ),
        name="strips",
    )(*operands)


def ring_tables(n_row, n_col, per_share):
    ring = list(range(0, n_row, 2)) + list(range(n_row - 1, 0, -2))
    table = np.zeros((n_row, n_row, per_share), np.int32)
    for place, row in enumerate(ring):
        for distance in range(n_row):
            turn, share = divmod(ring[(place - distance) % n_row], n_col)
            for q in range(per_share):
                table[row, distance, q] = (share * per_share + q) * (n_row // n_col) + turn
    forward = [(ring[p], ring[(p + 1) % n_row]) for p in range(n_row)]
    return forward, [(b, a) for a, b in forward], table


def ring_update(share, whole_diag, panel, trailing):
    n_row, n_col = lax.axis_size("row"), lax.axis_size("col")
    per_share = share.shape[0] // BLOCK
    forward, backward, table = ring_tables(n_row, n_col, per_share)
    columns = lax.dynamic_index_in_dim(
        jnp.asarray(table), lax.axis_index("row"), 0, keepdims=False
    )
    row_raw = lax.all_gather(panel, "col", axis=0, tiled=True)
    lower, inverse, panel_factor = factor(whole_diag, panel)
    share, inverse = lax.optimization_barrier((share, inverse))
    ahead = lax.ppermute(share, "row", forward)
    behind = lax.ppermute(share, "row", backward)
    left = make_left(row_raw, inverse)
    out = update_strips(columns[0], [share], left, inverse, trailing, None)
    ahead, behind, out = lax.optimization_barrier((ahead, behind, out))
    ready, numbers = [], []
    middle, half = n_row // 2, share.shape[0] // 2
    for distance in range(1, middle + 1):
        ready, numbers = ready + [ahead, behind], numbers + [distance, n_row - distance]
        if distance < middle - 1:
            ahead = lax.ppermute(ahead, "row", forward)
            behind = lax.ppermute(behind, "row", backward)
        elif distance == middle - 1:
            ahead = lax.ppermute(ahead[:half], "row", forward)
            behind = lax.ppermute(behind[half:], "row", backward)
        else:
            ready, numbers = [jnp.concatenate([ahead, behind])], [middle]
        wanted = jnp.concatenate([columns[number] for number in numbers])
        out = update_strips(wanted, ready, left, inverse, trailing, out)
        if distance < middle:
            ahead, behind, out = lax.optimization_barrier((ahead, behind, out))
        ready, numbers = [], []
    return lower, panel_factor, out


def per_device(diag_block, panel, trailing):
    n_row, n_col = lax.axis_size("row"), lax.axis_size("col")
    ratio = n_row // n_col
    swap = []
    for turn in range(ratio):
        for a in range(n_col):
            for b in range(n_col):
                source = (turn * n_col + a) * n_col + b
                swap.append((source, (turn * n_col + b) * n_col + a))
    whole_diag = gather_diag(diag_block, n_row, n_col)
    panel, whole_diag = lax.optimization_barrier((panel, whole_diag))
    column_share = lax.ppermute(panel, ("row", "col"), swap)
    if panel.shape[0] % BLOCK == 0 and n_row % 2 == 0 and n_row >= 4:
        lower, panel_factor, trailing_out = ring_update(
            column_share, whole_diag, panel, trailing
        )
    else:
        column_raw = lax.all_gather(column_share, "row", axis=0, tiled=True)
        row_raw = lax.all_gather(panel, "col", axis=0, tiled=True)
        lower, inverse, panel_factor = factor(whole_diag, panel)
        trailing_out = update(row_raw, column_raw, inverse, trailing, ratio)
    share = diag_block.shape[0]
    me = lax.axis_index(("row", "col"))
    factor_rows = lax.dynamic_slice_in_dim(lower, me * share, share, 0)
    return (factor_rows, panel_factor, trailing_out)


def solution(mesh):
    placed = (P(("row", "col"), None), P(("row", "col"), None), P("row", "col"))
    return jax.shard_map(
        per_device,
        mesh=mesh,
        in_specs=placed,
        out_specs=placed,
        check_vma=False,
    )
```
